256 devices in a mesh: row: 8 (over z), col: 32 (over x, y, core).
Axes of the slice: x: 4, y: 4, z: 8, core: 2. Of those that a mesh axis runs over, the one named last changes fastest.
Arguments:
- gradient: bfloat16 [16384, 16384], P('row', 'col'), may hold values from -6 to 6
- momentum: bfloat16 [16384, 16384], P('row', 'col'), may hold values from -6 to 6
- right_factor: float32 [16384, 256], P('col'), may hold values from -12 to 12
- weight: bfloat16 [16384, 16384], P('row', 'col'), may hold values from -6 to 6
Outputs:
- new_weight: bfloat16 [16384, 16384], P('row', 'col')
- new_momentum: bfloat16 [16384, 16384], P('row', 'col')
- new_factor: float32 [16384, 256], P('col')
The draws below stay inside these ranges and needn't reach their ends.
All inputs are finite; a program needn't handle non-finite values.
Results may differ from the reference program's by a relative error of at most 0.015.
Values may be sent and summed in bfloat16 or wider, within the bound.
A program may use at most 64 MiB of HBM per device.

```python
import jax
import jax.numpy as jnp
from jax import lax

ROWS = 16384
COLS = 16384
RANK = 256


def draw_right_factor(key, part):
    key = jax.random.fold_in(key, 7)
    scale_key = jax.random.fold_in(key, 1)
    own_key = jax.random.fold_in(key, 2)
    column_scale = jnp.exp(jax.random.uniform(scale_key, (1, RANK), jnp.float32, 0.0, 1.0986))
    own = jnp.clip(jax.random.normal(own_key, (COLS, RANK), jnp.float32), -4.0, 4.0)
    return own * column_scale


def steps_of(rng, dims, shards, low, largest):
    def one(position, shards_of):
        draws = jax.random.uniform(jax.random.fold_in(jax.random.fold_in(rng, 6), position), (shards_of,), jnp.float32, low / len(shards), largest / len(shards))
        return jnp.repeat(jnp.exp(draws), dims[position] // shards_of).reshape((-1,) + (1,) * (len(dims) - position - 1))

    factor_of = one(*shards[0])
    for cut in shards[1:]:
        factor_of = factor_of * one(*cut)
    return factor_of


def scatter_about(stream_key, shape, spread, most, split=(), held_as=jnp.bfloat16):
    array = jax.random.normal(stream_key, shape, jnp.float32) * spread
    if len(split) > 0:
        array = steps_of(stream_key, shape, split, -0.22, 0.18) * array
    return jnp.clip(array, min=-most, max=most).astype(held_as)


def setup_inputs(seed: int = 0) -> dict:
    splits = jax.random.split(jax.random.key(seed), 5)
    return {
        "gradient": scatter_about(splits[0], (ROWS, COLS), 1.0, 6.0, ((0, 8), (1, 32))),
        "momentum": scatter_about(splits[1], (ROWS, COLS), 1.0, 6.0, ((0, 8), (1, 32))),
        "right_factor": draw_right_factor(jax.random.fold_in(splits[4], 71), 0),
        "weight": scatter_about(splits[3], (ROWS, COLS), 1.0, 6.0, ((0, 8), (1, 32))),
    }


momentum_keep = 0.6
step_size = 0.1

def contract_rows(first, second, exact):
    if exact:
        return lax.dot_general(first.astype(jnp.float32), second.astype(jnp.float32), (((0,), (0,)), ((), ())), precision=lax.Precision.HIGHEST, preferred_element_type=jnp.float32)
    return lax.dot_general(first.astype(jnp.float32), second.astype(jnp.float32), (((0,), (0,)), ((), ())), preferred_element_type=jnp.float32)

def cholesky_pass(left):
    gram = contract_rows(left, left, True)
    lower = jnp.linalg.cholesky(gram)
    return lax.linalg.triangular_solve(lower, left, left_side=False, lower=True, transpose_a=True)

def reference(gradient, momentum, right_factor, weight):
    blended = (momentum.astype(jnp.float32) + gradient.astype(jnp.float32)).astype(jnp.bfloat16)
    left = jnp.dot(blended.astype(jnp.float32), right_factor.astype(jnp.bfloat16).astype(jnp.float32), preferred_element_type=jnp.float32)
    ortho = cholesky_pass(left)
    left_half = ortho.astype(jnp.bfloat16)
    right = contract_rows(blended, left_half, False)
    column_mean = lax.optimization_barrier(jnp.sum(right * right, axis=0)) / COLS
    new_factor = right * lax.rsqrt(column_mean + 1e-06)
    right_half = right.astype(jnp.bfloat16)
    projection = jnp.dot(left_half.astype(jnp.float32), right_half.T.astype(jnp.float32), preferred_element_type=jnp.float32)
    new_momentum = (blended.astype(jnp.float32) - (1.0 - momentum_keep) * projection).astype(jnp.bfloat16)
    new_half = new_factor.astype(jnp.bfloat16)
    direction = jnp.dot(left_half.astype(jnp.float32), new_half.T.astype(jnp.float32), preferred_element_type=jnp.float32)
    scaled = step_size * (ROWS / RANK) ** 0.5
    new_weight = (weight.astype(jnp.float32) - scaled * direction).astype(jnp.bfloat16)
    return (new_weight, new_momentum, new_factor)
```

```python
import functools

import jax
import jax.numpy as jnp
from jax import lax
from jax.experimental import pallas as pl
from jax.experimental.pallas import tpu as pltpu
from jax.sharding import PartitionSpec as P

ROWS = 16384
COLS = 16384
RANK = 256
CORES = 2
NX = 4
NY = 4

momentum_keep = 0.6
step_size = 0.1

F32 = jnp.float32
BF16 = jnp.bfloat16
MESH = pl.DeviceIdType.MESH


def split3(value):
    high = value.astype(BF16)
    rest = value - high.astype(F32)
    middle = rest.astype(BF16)
    return high, middle, (rest - middle.astype(F32)).astype(BF16)


def inverse_factor(gram_ref, work_ref, out_ref, size=32, group=16):
    n = gram_ref.shape[0]
    tiles_across = n // 128
    gram = gram_ref[...]
    rows = lax.broadcasted_iota(jnp.int32, (n, n), 0)
    cols = lax.broadcasted_iota(jnp.int32, (n, n), 1)
    diagonal = jnp.where(rows == cols, gram, 0.0)
    scale_row = lax.rsqrt(jnp.sum(diagonal, axis=0, keepdims=True))
    scale_col = lax.rsqrt(jnp.sum(diagonal, axis=1, keepdims=True))
    work_ref[:, :n] = gram * scale_row * scale_col
    work_ref[:, n:] = jnp.where(rows == cols, 1.0, 0.0)

    def block(j, carry):
        start = pl.multiple_of(j * size, size)
        outer = pl.multiple_of((j // (128 // size)) * 128, 128)
        lead = work_ref[pl.ds(start, size), pl.ds(outer, 128)]
        lead = pltpu.roll(lead, lax.rem(128 - (start - outer), 128), 1)
        panel = work_ref[pl.ds(start, size), :]
        tiles = [lead] + [panel[:, t * 128 : (t + 1) * 128] for t in range(2 * tiles_across)]
        done = []
        for first in range(0, size, group):
            height = size - first
            sub = lax.broadcasted_iota(jnp.int32, (height, 128), 0)
            top = sub[:group]
            lead = tiles[0]
            columns = [
                jnp.broadcast_to(lead[:, first + i : first + i + 1], (height, 128))
                for i in range(group)
            ]
            scale = jnp.ones((group, 128), F32)
            for k in range(0, group, 2):
                one, two = columns[k], columns[k + 1]
                a = one[k : k + 1, :]
                b = one[k + 1 : k + 2, :]
                c = two[k + 1 : k + 2, :]
                det = a * c - b * b
                inv_a = 1.0 / a
                inv_det = 1.0 / det
                m1 = (one * c - two * b) * inv_det
                m2 = (two * a - one * b) * inv_det
                m1 = jnp.where(sub > k + 1, m1, jnp.where(sub == k + 1, b * inv_a, 0.0))
                m2 = jnp.where(sub > k + 1, m2, 0.0)
                scale = jnp.where(
                    top == k,
                    lax.rsqrt(a),
                    jnp.where(top == k + 1, lax.rsqrt(det * inv_a), scale),
                )
                for i in range(k + 2, group):
                    old = columns[i]
                    columns[i] = old - m1 * old[k : k + 1, :] - m2 * old[k + 1 : k + 2, :]
                tiles = [t - m1 * t[k : k + 1, :] - m2 * t[k + 1 : k + 2, :] for t in tiles]
            done.append([t[:group] * scale for t in tiles[1:]])
            tiles = [t[group:] for t in tiles]
        tiles = [jnp.concatenate([d[t] for d in done], axis=0) for t in range(2 * tiles_across)]
        left = jnp.concatenate(tiles[:tiles_across], axis=1)
        right = jnp.concatenate(tiles[tiles_across:], axis=1)
        out_ref[pl.ds(start, size), :] = right * scale_row

        @pl.when(j < n // size - 1)
        def _():
            lane = lax.broadcasted_iota(jnp.int32, (size, n), 1)
            rest = jnp.where(lane >= start + size, left, 0.0)
            ph, pm, pq = split3(rest)
            xh, xm, xq = split3(right)
            lhs = jnp.concatenate([ph, ph, pm, pm, ph, pq], axis=0)
            rhs_g = jnp.concatenate([ph, pm, ph, pm, pq, ph], axis=0)
            rhs_x = jnp.concatenate([xh, xm, xh, xm, xq, xh], axis=0)
            rhs = jnp.concatenate([rhs_g, rhs_x], axis=1)
            work_ref[...] -= lax.dot_general(
                lhs, rhs, (((0,), (0,)), ((), ())), preferred_element_type=F32
            )

        return carry

    lax.fori_loop(0, n // size, block, 0)


def factor_kernel(
    nx,
    ny,
    nz,
    cols_total,
    g_hbm,
    m_hbm,
    v_hbm,
    la_out,
    lb_out,
    z1_out,
    z2_out,
    nf_out,
    g_v,
    m_v,
    v_v,
    b_v,
    xs,
    xr,
    s_v,
    sa,
    sb,
    ra1,
    rb1,
    ta,
    tb,
    ta_h,
    tb_h,
    ra2,
    rb2,
    la,
    lb,
    gfull,
    gz,
    gall,
    wh,
    wr,
    wg,
    work,
    inv,
    cs,
    z1,
    z2,
    nf,
    load_sem,
    out_sem,
    pair_s,
    pair_r,
    a1_s,
    a1_r,
    b1_s,
    b1_r,
    a2_s,
    a2_r,
    b2_s,
    b2_r,
    ga1_s,
    ga1_r,
    gb1_s,
    gb1_r,
    ga2_s,
    ga2_r,
    gb2_s,
    gb2_r,
    fa_s,
    fa_r,
    fb_s,
    fb_r,
    gz_s,
    gz_r,
    gp_s,
    gp_r,
    wr_s,
    wr_r,
    wg_s,
    wg_r,
    cs_s,
    cs_r,
):
    z = lax.axis_index("row")
    p = lax.axis_index("col")
    core = lax.rem(p, CORES)
    y = lax.rem(p // CORES, ny)
    x = p // (CORES * ny)
    plane = nx * ny * CORES
    rank = v_v.shape[1]
    half_rank = rank // 2
    half = b_v.shape[0] // CORES
    quarter = half // 2

    def at(x_to, y_to, core_to):
        return {"row": z, "col": (x_to * ny + y_to) * CORES + core_to}

    def send(src, dst, s_sem, r_sem, to):
        return pltpu.make_async_remote_copy(
            src_ref=src, dst_ref=dst, send_sem=s_sem, recv_sem=r_sem,
            device_id=to, device_id_type=MESH,
        )

    offsets = [(1 - core) * half, (1 - core) * half + quarter, core * half, core * half + quarter]
    offsets = [pl.multiple_of(o, quarter) for o in offsets]
    v_load = pltpu.make_async_copy(v_hbm, v_v, load_sem.at[8])
    v_load.start()
    loads = []
    for q, offset in enumerate(offsets):
        part = pl.ds(offset, quarter)
        pair = [
            pltpu.make_async_copy(g_hbm.at[part], g_v.at[part], load_sem.at[2 * q]),
            pltpu.make_async_copy(m_hbm.at[part], m_v.at[part], load_sem.at[2 * q + 1]),
        ]
        for c in pair:
            c.start()
        loads.append(pair)

    barrier = pltpu.get_barrier_semaphore()

    def greet_plane(d, carry):
        pl.semaphore_signal(
            barrier, inc=1, device_id={"row": z, "col": lax.rem(p + d, plane)}, device_id_type=MESH
        )
        return carry

    def greet_line(d, carry):
        pl.semaphore_signal(
            barrier, inc=1, device_id={"row": lax.rem(z + d, nz), "col": p}, device_id_type=MESH
        )
        return carry

    lax.fori_loop(1, plane, greet_plane, 0)
    lax.fori_loop(1, nz, greet_line, 0)

    v_load.wait()
    factor_half = v_v[...].astype(BF16)
    pair_copies = []
    for q, offset in enumerate(offsets):
        for c in loads[q]:
            c.wait()
        part = pl.ds(offset, quarter)
        blended = (m_v[part, :].astype(F32) + g_v[part, :].astype(F32)).astype(BF16)
        b_v[part, :] = blended
        product = jnp.dot(blended, factor_half, preferred_element_type=F32)
        if q < 2:
            xs[q] = product.astype(BF16)
            if q == 0:
                pl.semaphore_wait(barrier, plane - 1 + nz - 1)
            copy = send(xs.at[q], xr.at[q], pair_s.at[q], pair_r.at[q], at(x, y, 1 - core))
            copy.start()
            pair_copies.append(copy)
        else:
            s_v[pl.ds((q - 2) * quarter, quarter), :] = product

    chunk = half // (nx * ny)
    slab = chunk * ny
    for q in range(2):
        pair_copies[q].wait_recv()
        total = s_v[pl.ds(q * quarter, quarter), :] + xr[q].astype(F32)
        s_v[pl.ds(q * quarter, quarter), :] = total
        per = nx // 2
        for i in range(per):
            xi = q * per + i
            rows = total[i * slab : (i + 1) * slab, :].astype(BF16)
            sa[xi] = rows[:, :half_rank].reshape(ny, chunk, half_rank)
            sb[:, xi] = rows[:, half_rank:].reshape(ny, chunk, half_rank)
    a1, b1 = [], []
    for d in range(1, nx):
        to = lax.rem(x + d, nx)
        c = send(sa.at[to], ra1.at[d - 1], a1_s.at[d - 1], a1_r.at[d - 1], at(to, y, core))
        c.start()
        a1.append(c)
    for d in range(1, ny):
        to = lax.rem(y + d, ny)
        c = send(sb.at[to], rb1.at[d - 1], b1_s.at[d - 1], b1_r.at[d - 1], at(x, to, core))
        c.start()
        b1.append(c)
    acc = s_v[pl.ds(pl.multiple_of(x * slab, slab), slab), :half_rank].reshape(ny, chunk, half_rank)
    for d in range(1, nx):
        a1[d - 1].wait_recv()
        acc = acc + ra1[d - 1].astype(F32)
    ta[...] = acc
    ta_h[...] = acc.astype(BF16)
    a2, b2 = [], []
    for d in range(1, ny):
        to = lax.rem(y + d, ny)
        c = send(ta_h.at[to], ra2.at[d - 1], a2_s.at[d - 1], a2_r.at[d - 1], at(x, to, core))
        c.start()
        a2.append(c)
    for d in range(1, ny):
        b1[d - 1].wait_recv()
    for xi in range(nx):
        own = s_v[pl.ds(pl.multiple_of(xi * slab + y * chunk, chunk), chunk), half_rank:]
        for d in range(1, ny):
            own = own + rb1[d - 1, xi].astype(F32)
        tb[xi] = own
        tb_h[xi] = own.astype(BF16)
    for d in range(1, nx):
        to = lax.rem(x + d, nx)
        c = send(tb_h.at[to], rb2.at[d - 1], b2_s.at[d - 1], b2_r.at[d - 1], at(to, y, core))
        c.start()
        b2.append(c)

    acc = ta[y]
    for d in range(1, ny):
        a2[d - 1].wait_recv()
        acc = acc + ra2[d - 1].astype(F32)
    la[core, x, y] = acc.astype(BF16)
    ga1, gb1, ga2, gb2, fa, fb = [], [], [], [], [], []
    for d in range(1, ny):
        to = lax.rem(y + d, ny)
        here = la.at[core, x, y]
        c = send(here, here, ga1_s.at[d - 1], ga1_r.at[d - 1], at(x, to, core))
        c.start()
        ga1.append(c)
    acc = tb[x]
    for d in range(1, nx):
        b2[d - 1].wait_recv()
        acc = acc + rb2[d - 1].astype(F32)
    lb[core, x, y] = acc.astype(BF16)
    for d in range(1, nx):
        to = lax.rem(x + d, nx)
        here = lb.at[core, x, y]
        c = send(here, here, gb1_s.at[d - 1], gb1_r.at[d - 1], at(to, y, core))
        c.start()
        gb1.append(c)

    def forward_a(slot, x_of):
        here = la.at[core, x_of]
        c = send(here, here, fa_s.at[slot], fa_r.at[slot], at(x, y, 1 - core))
        c.start()
        fa.append(c)

    def forward_b(slot, y_of):
        here = lb.at[core, :, y_of]
        c = send(here, here, fb_s.at[slot], fb_r.at[slot], at(x, y, 1 - core))
        c.start()
        fb.append(c)

    for c in ga1:
        c.wait_recv()
    for d in range(1, nx):
        to = lax.rem(x + d, nx)
        here = la.at[core, x]
        c = send(here, here, ga2_s.at[d - 1], ga2_r.at[d - 1], at(to, y, core))
        c.start()
        ga2.append(c)
    forward_a(0, x)
    for c in gb1:
        c.wait_recv()
    for d in range(1, ny):
        to = lax.rem(y + d, ny)
        here = lb.at[core, :, y]
        c = send(here, here, gb2_s.at[d - 1], gb2_r.at[d - 1], at(x, to, core))
        c.start()
        gb2.append(c)
    forward_b(0, y)
    for d in range(1, max(nx, ny)):
        if d < nx:
            ga2[d - 1].wait_recv()
            forward_a(d, lax.rem(x + nx - d, nx))
        if d < ny:
            gb2[d - 1].wait_recv()
            forward_b(d, lax.rem(y + ny - d, ny))
    for c in fa + fb:
        c.wait_recv()

    outs = [
        pltpu.make_async_copy(la, la_out, out_sem.at[0]),
        pltpu.make_async_copy(lb, lb_out, out_sem.at[1]),
    ]
    for c in outs:
        c.start()

    n_rows = half * CORES
    left = jnp.concatenate(
        [la[...].reshape(n_rows, half_rank), lb[...].reshape(n_rows, half_rank)], axis=1
    )
    left_t = left.T
    gfull[...] = jnp.dot(left_t, left, preferred_element_type=F32)
    share = rank // plane
    mine = pl.ds(pl.multiple_of(p * share, share), share)
    gz[z] = gfull[mine, :]
    gz_c = []
    for d in range(1, nz):
        to = lax.rem(z + d, nz)
        c = send(gz.at[z], gz.at[z], gz_s.at[d - 1], gz_r.at[d - 1], {"row": to, "col": p})
        c.start()
        gz_c.append(c)

    w = jnp.dot(left_t, b_v[...], preferred_element_type=F32).astype(BF16)
    line = rank // nz
    wh[...] = w.reshape(nz, line, w.shape[1])
    wr[z] = wh[z]
    wr_c = []
    for d in range(1, nz):
        to = lax.rem(z + d, nz)
        c = send(wh.at[to], wr.at[z], wr_s.at[d - 1], wr_r.at[d - 1], {"row": to, "col": p})
        c.start()
        wr_c.append(c)

    for c in gz_c:
        c.wait_recv()
    acc = gz[0]
    for i in range(1, nz):
        acc = acc + gz[i]
    gall[mine, :] = acc

    def spread(d, carry):
        send(gall.at[mine], gall.at[mine], gp_s, gp_r, {"row": z, "col": lax.rem(p + d, plane)}).start()
        return carry

    lax.fori_loop(1, plane, spread, 0)

    for c in wr_c:
        c.wait_recv()
    acc = wr[0].astype(F32)
    for i in range(1, nz):
        acc = acc + wr[i].astype(F32)
    wg[z] = acc.astype(BF16)
    wg_c = []
    for d in range(1, nz):
        to = lax.rem(z + d, nz)
        c = send(wg.at[z], wg.at[z], wg_s.at[d - 1], wg_r.at[d - 1], {"row": to, "col": p})
        c.start()
        wg_c.append(c)

    others = gall.at[pl.ds(0, (plane - 1) * share)]
    all_gram = send(others, others, gp_s, gp_r, at(x, y, 1 - core))
    all_gram.wait_recv()
    inverse_factor(gall, work, inv)

    for c in wg_c:
        c.wait_recv()
    w = wg[...].reshape(rank, w.shape[1])
    high, middle, _ = split3(inv[...])
    right_t = jnp.dot(high, w, preferred_element_type=F32) + jnp.dot(
        middle, w, preferred_element_type=F32
    )
    squares = right_t * right_t
    sq_h, sq_m, _ = split3(squares)
    ones = jnp.ones((8, w.shape[1]), BF16)
    dims = (((1,), (1,)), ((), ()))
    cs[p] = lax.dot_general(ones, sq_h, dims, preferred_element_type=F32) + lax.dot_general(
        ones, sq_m, dims, preferred_element_type=F32
    )

    def spread_sums(d, carry):
        send(cs.at[p], cs.at[p], cs_s, cs_r, {"row": z, "col": lax.rem(p + d, plane)}).start()
        return carry

    lax.fori_loop(1, plane, spread_sums, 0)
    inv_t = inv[...].T
    right_half = right_t.astype(BF16)
    z1[...] = jnp.dot(inv_t.astype(BF16), right_half, preferred_element_type=F32).astype(BF16)
    right = right_t.T
    other_sums = cs.at[pl.ds(0, plane - 1)]
    all_sums = send(other_sums, other_sums, cs_s, cs_r, at(x, y, 1 - core))
    all_sums.wait_recv()
    acc = cs[0]
    for i in range(1, plane):
        acc = acc + cs[i]
    scale = lax.rsqrt(acc / cols_total + 1e-06)[0:1, :]
    z2[...] = jnp.dot(
        (inv_t * scale).astype(BF16), right_half, preferred_element_type=F32
    ).astype(BF16)
    nf[...] = right * scale
    last = [
        pltpu.make_async_copy(z1, z1_out, out_sem.at[2]),
        pltpu.make_async_copy(z2, z2_out, out_sem.at[3]),
        pltpu.make_async_copy(nf, nf_out, out_sem.at[4]),
    ]
    for c in last:
        c.start()
    for c in outs + last:
        c.wait()
    for c in pair_copies + a1 + b1 + a2 + b2 + ga1 + gb1 + ga2 + gb2 + fa + fb + gz_c + wr_c + wg_c:
        c.wait_send()
    all_gram.wait_send()
    all_sums.wait_send()


def update_kernel(scaled, g_ref, m_ref, w_ref, la_ref, lb_ref, z1_ref, z2_ref, nf_ref, nw_ref, nm_ref, out_ref):
    blended = (m_ref[...].astype(F32) + g_ref[...].astype(F32)).astype(BF16)
    left = jnp.concatenate([la_ref[...], lb_ref[...]], axis=1)
    projection = jnp.dot(left, z1_ref[...], preferred_element_type=F32)
    nm_ref[...] = (blended.astype(F32) - (1.0 - momentum_keep) * projection).astype(BF16)
    direction = jnp.dot(left, z2_ref[...], preferred_element_type=F32)
    nw_ref[...] = (w_ref[...].astype(F32) - scaled * direction).astype(BF16)
    out_ref[...] = nf_ref[...]


def local(nx, ny, nz, cols_total, scaled, gradient, momentum, right_factor, weight):
    n_rows, n_cols = gradient.shape
    rank = right_factor.shape[1]
    half_rank = rank // 2
    half = n_rows // CORES
    quarter = half // 2
    chunk = half // (nx * ny)
    plane = nx * ny * CORES
    share = rank // plane
    line = rank // nz
    any_spec = pl.BlockSpec(memory_space=pl.ANY)
    dma = pltpu.SemaphoreType.DMA
    vm = pltpu.VMEM
    scratch = [
        vm((n_rows, n_cols), BF16),
        vm((n_rows, n_cols), BF16),
        vm((n_cols, rank), F32),
        vm((n_rows, n_cols), BF16),
        vm((2, quarter, rank), BF16),
        vm((2, quarter, rank), BF16),
        vm((half, rank), F32),
        vm((nx, ny, chunk, half_rank), BF16),
        vm((ny, nx, chunk, half_rank), BF16),
        vm((nx - 1, ny, chunk, half_rank), BF16),
        vm((ny - 1, nx, chunk, half_rank), BF16),
        vm((ny, chunk, half_rank), F32),
        vm((nx, chunk, half_rank), F32),
        vm((ny, chunk, half_rank), BF16),
        vm((nx, chunk, half_rank), BF16),
        vm((ny - 1, chunk, half_rank), BF16),
        vm((nx - 1, chunk, half_rank), BF16),
        vm((CORES, nx, ny, chunk, half_rank), BF16),
        vm((CORES, nx, ny, chunk, half_rank), BF16),
        vm((rank, rank), F32),
        vm((nz, share, rank), F32),
        vm((rank, rank), F32),
        vm((nz, line, n_cols), BF16),
        vm((nz, line, n_cols), BF16),
        vm((nz, line, n_cols), BF16),
        vm((rank, 2 * rank), F32),
        vm((rank, rank), F32),
        vm((plane, 8, rank), F32),
        vm((rank, n_cols), BF16),
        vm((rank, n_cols), BF16),
        vm((n_cols, rank), F32),
        dma((9,)),
        dma((5,)),
        dma((2,)), dma((2,)),
        dma((nx - 1,)), dma((nx - 1,)), dma((ny - 1,)), dma((ny - 1,)),
        dma((ny - 1,)), dma((ny - 1,)), dma((nx - 1,)), dma((nx - 1,)),
        dma((ny - 1,)), dma((ny - 1,)), dma((nx - 1,)), dma((nx - 1,)),
        dma((nx - 1,)), dma((nx - 1,)), dma((ny - 1,)), dma((ny - 1,)),
        dma((nx,)), dma((nx,)), dma((ny,)), dma((ny,)),
        dma((nz - 1,)), dma((nz - 1,)),
        dma, dma,
        dma((nz - 1,)), dma((nz - 1,)),
        dma((nz - 1,)), dma((nz - 1,)),
        dma, dma,
    ]
    gathered = jax.ShapeDtypeStruct((CORES, nx, ny, chunk, half_rank), BF16)
    thin = jax.ShapeDtypeStruct((rank, n_cols), BF16)
    la, lb, z1, z2, nf = pl.pallas_call(
        functools.partial(factor_kernel, nx, ny, nz, cols_total),
        out_shape=[gathered, gathered, thin, thin, jax.ShapeDtypeStruct((n_cols, rank), F32)],
        in_specs=[any_spec] * 3,
        out_specs=[any_spec] * 5,
        scratch_shapes=scratch,
        compiler_params=pltpu.CompilerParams(
            collective_id=0, has_side_effects=True, vmem_limit_bytes=32 * 1024 * 1024
        ),
        name="factors",
    )(gradient, momentum, right_factor)
    la = la.reshape(n_rows, half_rank)
    lb = lb.reshape(n_rows, half_rank)
    steps = 8
    block = n_rows // steps
    piece = n_cols // steps
    rows_spec = pl.BlockSpec((block, n_cols), lambda i: (i, 0))
    left_spec = pl.BlockSpec((block, half_rank), lambda i: (i, 0))
    whole = pl.BlockSpec((rank, n_cols), lambda i: (0, 0))
    nf_spec = pl.BlockSpec((piece, rank), lambda i: (i, 0))
    return pl.pallas_call(
        functools.partial(update_kernel, scaled),
        grid=(steps,),
        out_shape=[
            jax.ShapeDtypeStruct((n_rows, n_cols), BF16),
            jax.ShapeDtypeStruct((n_rows, n_cols), BF16),
            jax.ShapeDtypeStruct((n_cols, rank), F32),
        ],
        in_specs=[rows_spec] * 3 + [left_spec] * 2 + [whole] * 2 + [nf_spec],
        out_specs=[rows_spec, rows_spec, nf_spec],
        compiler_params=pltpu.CompilerParams(vmem_limit_bytes=24 * 1024 * 1024),
        name="update",
    )(gradient, momentum, weight, la, lb, z1, z2, nf)


def build(mesh, nx, ny, nz, cols_total, rows_total, rank):
    scaled = step_size * (rows_total / rank) ** 0.5
    return jax.shard_map(
        functools.partial(local, nx, ny, nz, cols_total, scaled),
        mesh=mesh,
        in_specs=(P("row", "col"), P("row", "col"), P("col", None), P("row", "col")),
        out_specs=(P("row", "col"), P("row", "col"), P("col", None)),
        check_vma=False,
    )


def solution(mesh):
    return build(mesh, NX, NY, mesh.shape["row"], COLS, ROWS, RANK)
```

```python
import functools

import jax
import jax.numpy as jnp
from jax import lax
from jax.experimental import pallas as pl
from jax.experimental.pallas import tpu as pltpu
from jax.sharding import PartitionSpec as P

ROWS = 16384
COLS = 16384
RANK = 256
CORES = 2
sum_pieces = 2
piece_rows = 16
steps = 8
NX = 4
NY = 4

momentum_keep = 0.6
step_size = 0.1

F32 = jnp.float32
BF16 = jnp.bfloat16
MESH = pl.DeviceIdType.MESH


def split3(value):
    high = value.astype(BF16)
    rest = value - high.astype(F32)
    middle = rest.astype(BF16)
    return high, middle, (rest - middle.astype(F32)).astype(BF16)


def inverse_factor(gram_ref, work_ref, out_ref, size=32, group=16):
    n = gram_ref.shape[0]
    tiles_across = n // 128
    gram = gram_ref[...]
    rows = lax.broadcasted_iota(jnp.int32, (n, n), 0)
    cols = lax.broadcasted_iota(jnp.int32, (n, n), 1)
    diagonal = jnp.where(rows == cols, gram, 0.0)
    scale_row = lax.rsqrt(jnp.sum(diagonal, axis=0, keepdims=True))
    scale_col = lax.rsqrt(jnp.sum(diagonal, axis=1, keepdims=True))
    work_ref[:, :n] = gram * scale_row * scale_col
    work_ref[:, n:] = jnp.where(rows == cols, 1.0, 0.0)

    def block(j, carry):
        start = pl.multiple_of(j * size, size)
        outer = pl.multiple_of((j // (128 // size)) * 128, 128)
        lead = work_ref[pl.ds(start, size), pl.ds(outer, 128)]
        lead = pltpu.roll(lead, lax.rem(128 - (start - outer), 128), 1)
        panel = work_ref[pl.ds(start, size), :]
        tiles = [lead] + [panel[:, t * 128 : (t + 1) * 128] for t in range(2 * tiles_across)]
        done = []
        for first in range(0, size, group):
            height = size - first
            sub = lax.broadcasted_iota(jnp.int32, (height, 128), 0)
            top = sub[:group]
            lead = tiles[0]
            columns = [
                jnp.broadcast_to(lead[:, first + i : first + i + 1], (height, 128))
                for i in range(group)
            ]
            scale = jnp.ones((group, 128), F32)
            for k in range(0, group, 2):
                one, two = columns[k], columns[k + 1]
                a = one[k : k + 1, :]
                b = one[k + 1 : k + 2, :]
                c = two[k + 1 : k + 2, :]
                det = a * c - b * b
                inv_a = 1.0 / a
                inv_det = 1.0 / det
                m1 = (one * c - two * b) * inv_det
                m2 = (two * a - one * b) * inv_det
                m1 = jnp.where(sub > k + 1, m1, jnp.where(sub == k + 1, b * inv_a, 0.0))
                m2 = jnp.where(sub > k + 1, m2, 0.0)
                scale = jnp.where(
                    top == k,
                    lax.rsqrt(a),
                    jnp.where(top == k + 1, lax.rsqrt(det * inv_a), scale),
                )
                for i in range(k + 2, group):
                    old = columns[i]
                    columns[i] = old - m1 * old[k : k + 1, :] - m2 * old[k + 1 : k + 2, :]
                tiles = [t - m1 * t[k : k + 1, :] - m2 * t[k + 1 : k + 2, :] for t in tiles]
            done.append([t[:group] * scale for t in tiles[1:]])
            tiles = [t[group:] for t in tiles]
        tiles = [jnp.concatenate([d[t] for d in done], axis=0) for t in range(2 * tiles_across)]
        left = jnp.concatenate(tiles[:tiles_across], axis=1)
        right = jnp.concatenate(tiles[tiles_across:], axis=1)
        out_ref[pl.ds(start, size), :] = right * scale_row

        @pl.when(j < n // size - 1)
        def _():
            lane = lax.broadcasted_iota(jnp.int32, (size, n), 1)
            rest = jnp.where(lane >= start + size, left, 0.0)
            ph, pm, pq = split3(rest)
            xh, xm, xq = split3(right)
            lhs = jnp.concatenate([ph, ph, pm, pm, ph, pq], axis=0)
            rhs_g = jnp.concatenate([ph, pm, ph, pm, pq, ph], axis=0)
            rhs_x = jnp.concatenate([xh, xm, xh, xm, xq, xh], axis=0)
            rhs = jnp.concatenate([rhs_g, rhs_x], axis=1)
            work_ref[...] -= lax.dot_general(
                lhs, rhs, (((0,), (0,)), ((), ())), preferred_element_type=F32
            )

        return carry

    lax.fori_loop(0, n // size, block, 0)


def factor_kernel(nx, ny, nz, cols_total, g_hbm, m_hbm, v_hbm, *refs):
    b_outs, l_outs, refs = refs[:steps], refs[steps : 2 * steps], refs[2 * steps :]
    z1_out, xt_out, r_out, r2_out, scale_out, g_v, m_v, v_v, b_v, xs, xr, s_v, sa, ra, la, *refs = refs
    lt, gfull, gz, gall, wacc, wh, wr, wg, work, inv, cs, z1, xt, right, scale_v, *refs = refs
    load_sem, out_sem, pair_s, pair_r, rs_s, rs_r, ag_s, ag_r, fw_s, fw_r, *refs = refs
    gz_s, gz_r, gp_s, gp_r, wr_s, wr_r, wg_s, wg_r, cs_s, cs_r = refs
    z = lax.axis_index("row")
    p = lax.axis_index("col")
    core = lax.rem(p, CORES)
    q = p // CORES
    chips = nx * ny
    plane = chips * CORES
    rank = v_v.shape[1]
    half_rank = rank // 2
    n_cols = b_v.shape[1]
    half = b_v.shape[0] // CORES
    n_pieces, piece = xs.shape[0], xs.shape[1]

    def at(chip_to, core_to):
        return {"row": z, "col": chip_to * CORES + core_to}

    sent = []

    def copy_to(src, dst, s_sem, r_sem, to):
        return pltpu.make_async_remote_copy(
            src_ref=src,
            dst_ref=dst,
            send_sem=s_sem,
            recv_sem=r_sem,
            device_id=to,
            device_id_type=MESH,
        )

    def send(src, dst, s_sem, r_sem, to):
        copy = copy_to(src, dst, s_sem, r_sem, to)
        copy.start()
        sent.append(copy)
        return copy

    barrier = pltpu.get_barrier_semaphore()

    def greet_plane(d, carry):
        to = {"row": z, "col": lax.rem(p + d, plane)}
        pl.semaphore_signal(barrier, inc=1, device_id=to, device_id_type=MESH)
        return carry

    def greet_line(d, carry):
        to = {"row": lax.rem(z + d, nz), "col": p}
        pl.semaphore_signal(barrier, inc=1, device_id=to, device_id_type=MESH)
        return carry

    lax.fori_loop(1, plane, greet_plane, 0)
    lax.fori_loop(1, nz, greet_line, 0)
    v_load = pltpu.make_async_copy(v_hbm, v_v, load_sem.at[0])
    v_load.start()
    offsets = [(1 - core) * half + h * piece for h in range(n_pieces)]
    offsets += [core * half + h * piece for h in range(n_pieces)]
    offsets = [pl.multiple_of(o, piece) for o in offsets]
    loads = []
    for i, offset in enumerate(offsets):
        part = pl.ds(offset, piece)
        pair = [
            pltpu.make_async_copy(g_hbm.at[part], g_v.at[part], load_sem.at[2 * i + 1]),
            pltpu.make_async_copy(m_hbm.at[part], m_v.at[part], load_sem.at[2 * i + 2]),
        ]
        for c in pair:
            c.start()
        loads.append(pair)
    v_load.wait()
    factor_half = v_v[...].astype(BF16)

    def product(i):
        for c in loads[i]:
            c.wait()
        part = pl.ds(offsets[i], piece)
        blended = (m_v[part, :].astype(F32) + g_v[part, :].astype(F32)).astype(BF16)
        b_v[part, :] = blended
        return jnp.dot(blended, factor_half, preferred_element_type=F32)

    for h in range(n_pieces):
        xs[h] = product(h).astype(BF16)
    pl.semaphore_wait(barrier, plane - 1 + nz - 1)
    pairs = []
    for h in range(n_pieces):
        pairs.append(send(xs.at[h], xr.at[h], pair_s.at[h], pair_r.at[h], at(q, 1 - core)))

    def spread_piece(h):
        def to_chip(d, carry):
            to = lax.rem(q + d, chips)
            copy_to(sa.at[h, to], ra.at[h, q], rs_s.at[h], rs_r.at[h], at(to, core)).start()
            return carry

        lax.fori_loop(1, chips, to_chip, 0)

    for h in range(n_pieces):
        own = product(n_pieces + h)
        ra[h, q] = jnp.zeros((piece_rows, rank), BF16)
        pairs[h].wait_recv()
        total = (own + xr[h].astype(F32)).reshape(chips, piece_rows, rank)
        s_v[h] = total
        sa[h] = total.astype(BF16)
        spread_piece(h)

    def gather_piece(h):
        def to_chip(d, carry):
            to = lax.rem(q + d, chips)
            here = la.at[core, h, q]
            copy_to(here, here, ag_s.at[h], ag_r.at[h], at(to, core)).start()
            return carry

        lax.fori_loop(1, chips, to_chip, 0)

    waits = []
    for h in range(n_pieces):
        slots = ra.at[h, pl.ds(0, chips - 1)]
        arrived = copy_to(slots, slots, rs_s.at[h], rs_r.at[h], at(q, 1 - core))
        arrived.wait_recv()
        waits.append(arrived)
        la[core, h, q] = (s_v[h, q] + jnp.sum(ra[h].astype(F32), axis=0)).astype(BF16)
        gather_piece(h)

    def accumulate(h):
        forwards[h].wait_recv()
        for c in range(CORES):
            rows = la[c, h].reshape(piece, rank)
            rows_t = rows.T
            first = (c * n_pieces + h) * piece
            lt[:, first : first + piece] = rows_t
            update = jnp.dot(rows_t, rows, preferred_element_type=F32)
            gfull[...] = update if h == 0 and c == 0 else gfull[...] + update

    def accumulate_right(h):
        for c in range(CORES):
            first = (c * n_pieces + h) * piece
            update = jnp.dot(
                lt[:, first : first + piece],
                b_v[first : first + piece, :],
                preferred_element_type=F32,
            )
            wacc[...] = update if h == 0 and c == 0 else wacc[...] + update

    forwards = []
    for h in range(n_pieces):
        slots = la.at[core, h, pl.ds(0, chips - 1)]
        arrived = copy_to(slots, slots, ag_s.at[h], ag_r.at[h], at(q, 1 - core))
        arrived.wait_recv()
        waits.append(arrived)
        here = la.at[core, h]
        forwards.append(send(here, here, fw_s.at[h], fw_r.at[h], at(q, 1 - core)))
        if h > 0:
            accumulate(h - 1)
    for h in range(n_pieces - 1):
        accumulate_right(h)
    accumulate(n_pieces - 1)

    share = rank // plane
    mine = pl.ds(pl.multiple_of(p * share, share), share)
    gz[z] = gfull[mine, :]
    gz_c = []
    for d in range(1, nz):
        to = {"row": lax.rem(z + d, nz), "col": p}
        gz_c.append(send(gz.at[z], gz.at[z], gz_s.at[d - 1], gz_r.at[d - 1], to))

    accumulate_right(n_pieces - 1)
    w = wacc[...].astype(BF16)
    line = rank // nz
    part = line // sum_pieces
    wh[...] = w.reshape(nz, sum_pieces, part, n_cols)
    wr_c = []
    for h in range(sum_pieces):
        wr[h, z] = wh[z, h]
        for d in range(1, nz):
            to = lax.rem(z + d, nz)
            sems = wr_s.at[h, d - 1], wr_r.at[h, d - 1]
            wr_c.append(send(wh.at[to, h], wr.at[h, z], *sems, {"row": to, "col": p}))
    outs = []
    for i in range(steps):
        rows = b_v.shape[0] // steps
        c, h = i * rows // half, (i * rows % half) // piece
        chip = (i * rows % piece) // piece_rows
        source = la.at[c, h, pl.ds(chip, rows // piece_rows)]
        outs.append(pltpu.make_async_copy(source, l_outs[i], out_sem.at[2 * i]))
        source = b_v.at[pl.ds(i * rows, rows)]
        outs.append(pltpu.make_async_copy(source, b_outs[i], out_sem.at[2 * i + 1]))
    for c in outs:
        c.start()

    for c in gz_c:
        c.wait_recv()
    acc = gz[0]
    for i in range(1, nz):
        acc = acc + gz[i]
    gall[mine, :] = acc

    def spread(d, carry):
        to = {"row": z, "col": lax.rem(p + d, plane)}
        copy_to(gall.at[mine], gall.at[mine], gp_s, gp_r, to).start()
        return carry

    lax.fori_loop(1, plane, spread, 0)

    wg_c = []
    for h in range(sum_pieces):
        for c in wr_c[h * (nz - 1) : (h + 1) * (nz - 1)]:
            c.wait_recv()
        acc = wr[h, 0].astype(F32)
        for i in range(1, nz):
            acc = acc + wr[h, i].astype(F32)
        wg[z, h] = acc.astype(BF16)
        for d in range(1, nz):
            to = {"row": lax.rem(z + d, nz), "col": p}
            sems = wg_s.at[h, d - 1], wg_r.at[h, d - 1]
            wg_c.append(send(wg.at[z, h], wg.at[z, h], *sems, to))

    others = gall.at[pl.ds(0, (plane - 1) * share)]
    all_gram = copy_to(others, others, gp_s, gp_r, at(q, 1 - core))
    all_gram.wait_recv()
    inverse_factor(gall, work, inv)
    inv_t = inv[...].T.astype(BF16)
    xt[...] = inv_t
    outs.append(pltpu.make_async_copy(xt, xt_out, out_sem.at[2 * steps]))
    outs[-1].start()

    for c in wg_c:
        c.wait_recv()
    w = wg[...].reshape(rank, n_cols)
    high, middle, _ = split3(inv[...])
    right_t = jnp.dot(high, w, preferred_element_type=F32) + jnp.dot(
        middle, w, preferred_element_type=F32
    )
    squares = right_t * right_t
    sq_h, sq_m, _ = split3(squares)
    ones = jnp.ones((8, n_cols), BF16)
    dims = (((1,), (1,)), ((), ()))
    sums = lax.dot_general(ones, sq_h, dims, preferred_element_type=F32) + lax.dot_general(
        ones, sq_m, dims, preferred_element_type=F32
    )
    upper = lax.broadcasted_iota(jnp.int32, (8, half_rank), 0) < 4
    cs[p] = jnp.where(upper, sums[:, :half_rank], sums[:, half_rank:])

    def spread_sums(d, carry):
        to = {"row": z, "col": lax.rem(p + d, plane)}
        copy_to(cs.at[p], cs.at[p], cs_s, cs_r, to).start()
        return carry

    lax.fori_loop(1, plane, spread_sums, 0)
    z1[...] = jnp.dot(inv_t, right_t.astype(BF16), preferred_element_type=F32).astype(BF16)
    right[...] = right_t.T
    mid = n_cols // 2
    outs += [
        pltpu.make_async_copy(z1, z1_out, out_sem.at[2 * steps + 1]),
        pltpu.make_async_copy(right.at[pl.ds(0, mid)], r_out, out_sem.at[2 * steps + 2]),
        pltpu.make_async_copy(right.at[pl.ds(mid, mid)], r2_out, out_sem.at[2 * steps + 3]),
    ]
    for c in outs[-3:]:
        c.start()
    for c in sent + waits + [all_gram]:
        c.wait_send()
    other_sums = cs.at[pl.ds(0, plane - 1)]
    all_sums = copy_to(other_sums, other_sums, cs_s, cs_r, at(q, 1 - core))
    all_sums.wait_recv()
    acc = cs[0]
    for i in range(1, plane):
        acc = acc + cs[i]
    acc = lax.rsqrt(acc / cols_total + 1e-06)
    scale = jnp.concatenate([acc[0:1, :], acc[4:5, :]], axis=1)
    scale_v[...] = jnp.broadcast_to(scale, scale_v.shape)
    outs.append(pltpu.make_async_copy(scale_v, scale_out, out_sem.at[2 * steps + 4]))
    outs[-1].start()
    for c in outs:
        c.wait()
    all_sums.wait_send()


def update_kernel(scaled, *refs):
    b_refs, l_refs, refs = refs[:steps], refs[steps : 2 * steps], refs[2 * steps :]
    w_ref, z1_ref, xt_ref, r_ref, r2_ref, scale_ref, nw_hbm, nm_hbm, nf_hbm, nw, nm, nf, sems = refs
    block = nw.shape[0] // steps
    mid = r_ref.shape[0]
    scale = scale_ref[0:1, :]
    nf[:mid, :] = r_ref[...] * scale
    nf[mid:, :] = r2_ref[...] * scale
    copies = [pltpu.make_async_copy(nf, nf_hbm, sems.at[2 * steps])]
    copies[0].start()
    z2 = lax.dot_general(
        xt_ref[...],
        nf[...].astype(BF16),
        (((1,), (1,)), ((), ())),
        preferred_element_type=F32,
    ).astype(BF16)
    for i in range(steps):
        part = pl.ds(i * block, block)
        left = l_refs[i][...].reshape(block, z2.shape[0])
        projection = jnp.dot(left, z1_ref[...], preferred_element_type=F32)
        nm[part, :] = (b_refs[i][...].astype(F32) - (1.0 - momentum_keep) * projection).astype(BF16)
        copies.append(pltpu.make_async_copy(nm.at[part], nm_hbm.at[part], sems.at[2 * i]))
        copies[-1].start()
        direction = jnp.dot(left, z2, preferred_element_type=F32)
        nw[part, :] = (w_ref[part, :].astype(F32) - scaled * direction).astype(BF16)
        copies.append(pltpu.make_async_copy(nw.at[part], nw_hbm.at[part], sems.at[2 * i + 1]))
        copies[-1].start()
    for c in copies:
        c.wait()


def local(nx, ny, nz, cols_total, scaled, gradient, momentum, right_factor, weight):
    n_rows, n_cols = gradient.shape
    rank = right_factor.shape[1]
    half = n_rows // CORES
    chips = nx * ny
    piece = chips * piece_rows
    n_pieces = half // piece
    plane = chips * CORES
    share = rank // plane
    part = rank // nz // sum_pieces
    block = n_rows // steps
    any_spec = pl.BlockSpec(memory_space=pl.ANY)
    vm_spec = pl.BlockSpec(memory_space=pltpu.VMEM)
    dma = pltpu.SemaphoreType.DMA
    vm = pltpu.VMEM
    shape = jax.ShapeDtypeStruct
    rows = (n_pieces, chips, piece_rows, rank)
    scratch = [
        vm((n_rows, n_cols), BF16),
        vm((n_rows, n_cols), BF16),
        vm((n_cols, rank), F32),
        vm((n_rows, n_cols), BF16),
        vm((n_pieces, piece, rank), BF16),
        vm((n_pieces, piece, rank), BF16),
        vm(rows, F32),
        vm(rows, BF16),
        vm(rows, BF16),
        vm((CORES,) + rows, BF16),
        vm((rank, n_rows), BF16),
        vm((rank, rank), F32),
        vm((nz, share, rank), F32),
        vm((rank, rank), F32),
        vm((rank, n_cols), F32),
        vm((nz, sum_pieces, part, n_cols), BF16),
        vm((sum_pieces, nz, part, n_cols), BF16),
        vm((nz, sum_pieces, part, n_cols), BF16),
        vm((rank, 2 * rank), F32),
        vm((rank, rank), F32),
        vm((plane, 8, rank // 2), F32),
        vm((rank, n_cols), BF16),
        vm((rank, rank), BF16),
        vm((n_cols, rank), F32),
        vm((8, rank), F32),
        dma((4 * n_pieces + 1,)),
        dma((2 * steps + 5,)),
    ]
    scratch += [dma((n_pieces,))] * 8
    scratch += [dma((nz - 1,)), dma((nz - 1,)), dma, dma]
    scratch += [dma((sum_pieces, nz - 1))] * 4 + [dma, dma]
    outs = [shape((block, n_cols), BF16)] * steps
    outs += [shape((block // piece_rows, piece_rows, rank), BF16)] * steps
    outs += [shape((rank, n_cols), BF16), shape((rank, rank), BF16)]
    outs += [shape((n_cols // 2, rank), F32)] * 2 + [shape((8, rank), F32)]
    out = pl.pallas_call(
        functools.partial(factor_kernel, nx, ny, nz, cols_total),
        out_shape=outs,
        in_specs=[any_spec] * 3,
        out_specs=[any_spec] * len(outs),
        scratch_shapes=scratch,
        compiler_params=pltpu.CompilerParams(
            collective_id=0, has_side_effects=True, vmem_limit_bytes=51072 * 1024
        ),
        name="factors",
    )(gradient, momentum, right_factor)
    return pl.pallas_call(
        functools.partial(update_kernel, scaled),
        out_shape=[
            shape((n_rows, n_cols), BF16),
            shape((n_rows, n_cols), BF16),
            shape((n_cols, rank), F32),
        ],
        in_specs=[vm_spec] * (len(outs) + 1),
        out_specs=[any_spec] * 3,
        scratch_shapes=[
            vm((n_rows, n_cols), BF16),
            vm((n_rows, n_cols), BF16),
            vm((n_cols, rank), F32),
            dma((2 * steps + 1,)),
        ],
        compiler_params=pltpu.CompilerParams(vmem_limit_bytes=16 * 1024 * 1024),
        name="update",
    )(*out[: 2 * steps], weight, *out[2 * steps :])


def build(mesh, nx, ny, nz, cols_total, rows_total, rank):
    scaled = step_size * (rows_total / rank) ** 0.5
    return jax.shard_map(
        functools.partial(local, nx, ny, nz, cols_total, scaled),
        mesh=mesh,
        in_specs=(P("row", "col"), P("row", "col"), P("col", None), P("row", "col")),
        out_specs=(P("row", "col"), P("row", "col"), P("col", None)),
        check_vma=False,
    )


def solution(mesh):
    return build(mesh, NX, NY, mesh.shape["row"], COLS, ROWS, RANK)
```

```python
import functools

import jax
import jax.numpy as jnp
from jax import lax
from jax.experimental import pallas as pl
from jax.experimental.pallas import tpu as pltpu
from jax.sharding import PartitionSpec as P

ROWS = 16384
COLS = 16384
RANK = 256
CORES = 2
sum_pieces = 2
piece_rows = 16
steps = 8
NX = 4
NY = 4

momentum_keep = 0.6
step_size = 0.1

F32 = jnp.float32
BF16 = jnp.bfloat16
MESH = pl.DeviceIdType.MESH


def split3(value):
    high = value.astype(BF16)
    rest = value - high.astype(F32)
    middle = rest.astype(BF16)
    return high, middle, (rest - middle.astype(F32)).astype(BF16)


def inverse_factor(gram_ref, work_ref, out_ref, size=32, group=16):
    n = gram_ref.shape[0]
    tiles_across = n // 128
    gram = gram_ref[...]
    rows = lax.broadcasted_iota(jnp.int32, (n, n), 0)
    cols = lax.broadcasted_iota(jnp.int32, (n, n), 1)
    diagonal = jnp.where(rows == cols, gram, 0.0)
    scale_row = lax.rsqrt(jnp.sum(diagonal, axis=0, keepdims=True))
    scale_col = lax.rsqrt(jnp.sum(diagonal, axis=1, keepdims=True))
    work_ref[:, :n] = gram * scale_row * scale_col

    def block(start):
        outer = start // 128 * 128
        lead = work_ref[start : start + size, outer : outer + 128]
        if start != outer:
            lead = pltpu.roll(lead, 128 - (start - outer), 1)
        panel = work_ref[start : start + size, :]
        used = [t for t in range(tiles_across) if (t + 1) * 128 > start]
        used += [tiles_across + t for t in range(tiles_across) if t * 128 < start + size]
        tiles = [lead] + [panel[:, t * 128 : (t + 1) * 128] for t in used]
        done = []
        for first in range(0, size, group):
            lead = tiles[0]
            columns = [
                jnp.broadcast_to(lead[:, first + i : first + i + 1], (size - first, 128))
                for i in range(group)
            ]
            for base in range(0, group, 8):
                sub = lax.broadcasted_iota(jnp.int32, (size - first - base, 128), 0)
                top = sub[:8]
                scale = jnp.ones((8, 128), F32)
                for k in range(0, 8, 2):
                    one, two = columns[base + k], columns[base + k + 1]
                    a = one[k : k + 1, :]
                    b = one[k + 1 : k + 2, :]
                    c = two[k + 1 : k + 2, :]
                    det = a * c - b * b
                    inv_a = 1.0 / a
                    inv_det = 1.0 / det
                    m1 = (one * c - two * b) * inv_det
                    m2 = (two * a - one * b) * inv_det
                    m1 = jnp.where(sub > k + 1, m1, jnp.where(sub == k + 1, b * inv_a, 0.0))
                    m2 = jnp.where(sub > k + 1, m2, 0.0)
                    scale = jnp.where(
                        top == k,
                        lax.rsqrt(a),
                        jnp.where(top == k + 1, lax.rsqrt(det * inv_a), scale),
                    )
                    for i in range(base + k + 2, group):
                        old = columns[i]
                        columns[i] = old - m1 * old[k : k + 1, :] - m2 * old[k + 1 : k + 2, :]
                    tiles = [t - m1 * t[k : k + 1, :] - m2 * t[k + 1 : k + 2, :] for t in tiles]
                done.append([t[:8] * scale for t in tiles[1:]])
                tiles = [t[8:] for t in tiles]
                columns = [c[8:] if i >= base + 8 else c for i, c in enumerate(columns)]
        found = {t: jnp.concatenate([d[i] for d in done], axis=0) for i, t in enumerate(used)}
        empty = jnp.zeros((size, 128), F32)
        tiles = [found.get(t, empty) for t in range(2 * tiles_across)]
        left = jnp.concatenate(tiles[:tiles_across], axis=1)
        right = jnp.concatenate(tiles[tiles_across:], axis=1)
        out_ref[start : start + size, :] = right * scale_row

        if start + size < n:
            lane = lax.broadcasted_iota(jnp.int32, (size, n), 1)
            rest = jnp.where(lane >= start + size, left, 0.0)
            ph, pm, pq = split3(rest)
            xh, xm, xq = split3(right)
            lhs = jnp.concatenate([ph, ph, pm, pm, ph, pq], axis=0)
            rhs_g = jnp.concatenate([ph, pm, ph, pm, pq, ph], axis=0)
            rhs_x = jnp.concatenate([xh, xm, xh, xm, xq, xh], axis=0)
            rhs = jnp.concatenate([rhs_g, rhs_x], axis=1)
            under = (start + size) // 128 * 128
            work_ref[under:, :] -= lax.dot_general(
                lhs[:, under:], rhs, (((0,), (0,)), ((), ())), preferred_element_type=F32
            )

    for start in range(0, n, size):
        block(start)


def factor_kernel(nx, ny, nz, cols_total, g_hbm, m_hbm, v_hbm, *refs):
    nm_outs, l_outs, refs = refs[:steps], refs[steps : 2 * steps], refs[2 * steps :]
    xt_out, r_out, r2_out, scale_out, g_v, m_v, v_v, b_v, xs, xr, s_v, sa, ra, la, *refs = refs
    lt, gfull, gz, gall, wacc, wh, wr, wg, work, inv, cs, z1, xt, right, scale_v, *refs = refs
    load_sem, out_sem, pair_s, pair_r, rs_s, rs_r, ag_s, ag_r, fw_s, fw_r, *refs = refs
    gz_s, gz_r, gp_s, gp_r, wr_s, wr_r, wg_s, wg_r, cs_s, cs_r = refs
    z = lax.axis_index("row")
    p = lax.axis_index("col")
    core = lax.rem(p, CORES)
    q = p // CORES
    chips = nx * ny
    plane = chips * CORES
    rank = v_v.shape[1]
    half_rank = rank // 2
    n_cols = b_v.shape[1]
    half = b_v.shape[0] // CORES
    n_pieces, piece = xs.shape[0], xs.shape[1]

    def at(chip_to, core_to):
        return {"row": z, "col": chip_to * CORES + core_to}

    sent = []

    def copy_to(src, dst, s_sem, r_sem, to):
        return pltpu.make_async_remote_copy(
            src_ref=src,
            dst_ref=dst,
            send_sem=s_sem,
            recv_sem=r_sem,
            device_id=to,
            device_id_type=MESH,
        )

    def send(src, dst, s_sem, r_sem, to):
        copy = copy_to(src, dst, s_sem, r_sem, to)
        copy.start()
        sent.append(copy)
        return copy

    v_load = pltpu.make_async_copy(v_hbm, v_v, load_sem.at[0])
    v_load.start()
    offsets = [(1 - core) * half + h * piece for h in range(n_pieces)]
    offsets += [core * half + h * piece for h in range(n_pieces)]
    offsets = [pl.multiple_of(o, piece) for o in offsets]
    loads = []
    for i, offset in enumerate(offsets):
        part = pl.ds(offset, piece)
        pair = [
            pltpu.make_async_copy(g_hbm.at[part], g_v.at[part], load_sem.at[2 * i + 1]),
            pltpu.make_async_copy(m_hbm.at[part], m_v.at[part], load_sem.at[2 * i + 2]),
        ]
        for c in pair:
            c.start()
        loads.append(pair)
    barrier = pltpu.get_barrier_semaphore()

    def ring(here, d, size):
        to = here + d
        return jnp.where(to >= size, to - size, to)

    def greet_plane(d, carry):
        to = {"row": z, "col": ring(p, d, plane)}
        pl.semaphore_signal(barrier, inc=1, device_id=to, device_id_type=MESH)
        return carry

    def greet_line(d, carry):
        to = {"row": ring(z, d, nz), "col": p}
        pl.semaphore_signal(barrier, inc=1, device_id=to, device_id_type=MESH)
        return carry

    for d in range(1, nz):
        greet_line(d, 0)
    for d in range(1, plane):
        greet_plane(d, 0)
    v_load.wait()
    factor_half = v_v[...].astype(BF16)

    def product(i):
        for c in loads[i]:
            c.wait()
        part = pl.ds(offsets[i], piece)
        blended = (m_v[part, :].astype(F32) + g_v[part, :].astype(F32)).astype(BF16)
        b_v[part, :] = blended
        return jnp.dot(blended, factor_half, preferred_element_type=F32)

    for h in range(n_pieces):
        xs[h] = product(h).astype(BF16)
    for h in range(n_pieces):
        s_v[h] = product(n_pieces + h).reshape(chips, piece_rows, rank)
        ra[h, q] = jnp.zeros((piece_rows, rank), BF16)
    pl.semaphore_wait(barrier, plane - 1 + nz - 1)
    pairs = []
    for h in range(n_pieces):
        pairs.append(send(xs.at[h], xr.at[h], pair_s.at[h], pair_r.at[h], at(q, 1 - core)))

    def spread_piece(h):
        def to_chip(d, carry):
            to = ring(q, d, chips)
            copy_to(sa.at[h, to], ra.at[h, q], rs_s.at[h], rs_r.at[h], at(to, core)).start()
            return carry

        lax.fori_loop(1, chips, to_chip, 0)

    for h in range(n_pieces):
        pairs[h].wait_recv()
        total = s_v[h] + xr[h].astype(F32).reshape(chips, piece_rows, rank)
        s_v[h] = total
        sa[h] = total.astype(BF16)
        spread_piece(h)

    def gather_piece(h):
        def to_chip(d, carry):
            to = ring(q, d, chips)
            here = la.at[core, h, q]
            copy_to(here, here, ag_s.at[h], ag_r.at[h], at(to, core)).start()
            return carry

        lax.fori_loop(1, chips, to_chip, 0)

    waits = []
    for h in range(n_pieces):
        slots = ra.at[h, pl.ds(0, chips - 1)]
        arrived = copy_to(slots, slots, rs_s.at[h], rs_r.at[h], at(q, 1 - core))
        arrived.wait_recv()
        waits.append(arrived)
        la[core, h, q] = (s_v[h, q] + jnp.sum(ra[h].astype(F32), axis=0)).astype(BF16)
        gather_piece(h)

    def accumulate(h):
        forwards[h].wait_recv()
        for c in range(CORES):
            rows = la[c, h].reshape(piece, rank)
            rows_t = rows.T
            first = (c * n_pieces + h) * piece
            lt[:, first : first + piece] = rows_t
            update = jnp.dot(rows_t, rows, preferred_element_type=F32)
            gfull[...] = update if h == 0 and c == 0 else gfull[...] + update

    def accumulate_right(h):
        for c in range(CORES):
            first = (c * n_pieces + h) * piece
            update = jnp.dot(
                lt[:, first : first + piece],
                b_v[first : first + piece, :],
                preferred_element_type=F32,
            )
            wacc[...] = update if h == 0 and c == 0 else wacc[...] + update

    forwards = []
    for h in range(n_pieces):
        slots = la.at[core, h, pl.ds(0, chips - 1)]
        arrived = copy_to(slots, slots, ag_s.at[h], ag_r.at[h], at(q, 1 - core))
        arrived.wait_recv()
        waits.append(arrived)
        here = la.at[core, h]
        forwards.append(send(here, here, fw_s.at[h], fw_r.at[h], at(q, 1 - core)))
        if h > 0:
            accumulate(h - 1)
    for h in range(n_pieces - 1):
        accumulate_right(h)
    accumulate(n_pieces - 1)

    share = rank // plane
    mine = pl.ds(pl.multiple_of(p * share, share), share)
    gz[z] = gfull[mine, :]
    gz_c = []
    for d in range(1, nz):
        to = {"row": ring(z, d, nz), "col": p}
        gz_c.append(send(gz.at[z], gz.at[z], gz_s.at[d - 1], gz_r.at[d - 1], to))

    accumulate_right(n_pieces - 1)
    w = wacc[...].astype(BF16)
    line = rank // nz
    part = line // sum_pieces
    wh[...] = w.reshape(nz, sum_pieces, part, n_cols)
    wr_c = []
    for h in range(sum_pieces):
        wr[h, z] = wh[z, h]
        for d in range(1, nz):
            to = ring(z, d, nz)
            sems = wr_s.at[h, d - 1], wr_r.at[h, d - 1]
            wr_c.append(send(wh.at[to, h], wr.at[h, z], *sems, {"row": to, "col": p}))
    outs = []
    for i in range(steps):
        rows = b_v.shape[0] // steps
        c, h = i * rows // half, (i * rows % half) // piece
        chip = (i * rows % piece) // piece_rows
        source = la.at[c, h, pl.ds(chip, rows // piece_rows)]
        outs.append(pltpu.make_async_copy(source, l_outs[i], out_sem.at[2 * i]))
    for c in outs:
        c.start()

    for c in gz_c:
        c.wait_recv()
    acc = gz[0]
    for i in range(1, nz):
        acc = acc + gz[i]
    gall[mine, :] = acc

    def spread(d, carry):
        to = {"row": z, "col": ring(p, d, plane)}
        copy_to(gall.at[mine], gall.at[mine], gp_s, gp_r, to).start()
        return carry

    lax.fori_loop(1, plane, spread, 0)

    wg_c = []
    for h in range(sum_pieces):
        for c in wr_c[h * (nz - 1) : (h + 1) * (nz - 1)]:
            c.wait_recv()
        acc = wr[h, 0].astype(F32)
        for i in range(1, nz):
            acc = acc + wr[h, i].astype(F32)
        wg[z, h] = acc.astype(BF16)
        for d in range(1, nz):
            to = {"row": ring(z, d, nz), "col": p}
            sems = wg_s.at[h, d - 1], wg_r.at[h, d - 1]
            wg_c.append(send(wg.at[z, h], wg.at[z, h], *sems, to))

    others = gall.at[pl.ds(0, (plane - 1) * share)]
    at_row = lax.broadcasted_iota(jnp.int32, (rank, rank), 0)
    at_col = lax.broadcasted_iota(jnp.int32, (rank, rank), 1)
    work[:, rank:] = jnp.where(at_row == at_col, 1.0, 0.0)
    all_gram = copy_to(others, others, gp_s, gp_r, at(q, 1 - core))
    all_gram.wait_recv()
    inverse_factor(gall, work, inv)

    for c in wg_c:
        c.wait_recv()
    w = wg[...].reshape(rank, n_cols)
    high, middle, _ = split3(inv[...])
    right_t = jnp.dot(high, w, preferred_element_type=F32) + jnp.dot(
        middle, w, preferred_element_type=F32
    )
    squares = right_t * right_t
    sq_h, sq_m, _ = split3(squares)
    ones = jnp.ones((8, n_cols), BF16)
    dims = (((1,), (1,)), ((), ()))
    sums = lax.dot_general(ones, sq_h, dims, preferred_element_type=F32) + lax.dot_general(
        ones, sq_m, dims, preferred_element_type=F32
    )
    cs[p] = jnp.concatenate([sums[0:1, :half_rank], sums[0:1, half_rank:]], axis=0)

    def spread_sums(d, carry):
        to = {"row": z, "col": ring(p, d, plane)}
        copy_to(cs.at[p], cs.at[p], cs_s, cs_r, to).start()
        return carry

    lax.fori_loop(1, plane, spread_sums, 0)
    inv_t = inv[...].T.astype(BF16)
    xt[...] = inv_t
    z1[...] = jnp.dot(inv_t, right_t.astype(BF16), preferred_element_type=F32).astype(BF16)
    right[...] = right_t.T
    mid = n_cols // 2
    outs += [
        pltpu.make_async_copy(xt, xt_out, out_sem.at[2 * steps + 1]),
        pltpu.make_async_copy(right.at[pl.ds(0, mid)], r_out, out_sem.at[2 * steps + 2]),
        pltpu.make_async_copy(right.at[pl.ds(mid, mid)], r2_out, out_sem.at[2 * steps + 3]),
    ]
    for c in outs[-3:]:
        c.start()
    rows = b_v.shape[0] // steps
    for i in range(steps):
        c, h = i * rows // half, (i * rows % half) // piece
        chip = (i * rows % piece) // piece_rows
        part = pl.ds(i * rows, rows)
        left = la[c, h, chip : chip + rows // piece_rows].reshape(rows, rank)
        projection = jnp.dot(left, z1[...], preferred_element_type=F32)
        b_v[part, :] = (b_v[part, :].astype(F32) - (1.0 - momentum_keep) * projection).astype(BF16)
        outs.append(pltpu.make_async_copy(b_v.at[part], nm_outs[i], out_sem.at[2 * i + 1]))
        outs[-1].start()
    for c in sent + waits + [all_gram]:
        c.wait_send()
    other_sums = cs.at[pl.ds(0, plane - 1)]
    all_sums = copy_to(other_sums, other_sums, cs_s, cs_r, at(q, 1 - core))
    all_sums.wait_recv()
    acc = cs[0]
    for i in range(1, plane):
        acc = acc + cs[i]
    acc = lax.rsqrt(acc / cols_total + 1e-06)
    scale = jnp.concatenate([acc[0:1, :], acc[1:2, :]], axis=1)
    scale_v[...] = jnp.broadcast_to(scale, scale_v.shape)
    outs.append(pltpu.make_async_copy(scale_v, scale_out, out_sem.at[2 * steps + 4]))
    outs[-1].start()
    for c in outs:
        c.wait()
    all_sums.wait_send()


def update_kernel(scaled, *refs):
    nm_refs, l_refs, refs = refs[:steps], refs[steps : 2 * steps], refs[2 * steps :]
    w_ref, xt_ref, r_ref, r2_ref, scale_ref, nw_hbm, nm_hbm, nf_hbm, nw, nf, sems = refs
    block = nw.shape[0] // steps
    mid = r_ref.shape[0]
    copies = []
    for i in range(steps):
        part = pl.ds(i * block, block)
        copies.append(pltpu.make_async_copy(nm_refs[i], nm_hbm.at[part], sems.at[2 * i]))
        copies[-1].start()
    scale = scale_ref[0:1, :]
    nf[:mid, :] = r_ref[...] * scale
    nf[mid:, :] = r2_ref[...] * scale
    copies.append(pltpu.make_async_copy(nf, nf_hbm, sems.at[2 * steps]))
    copies[-1].start()
    z2 = lax.dot_general(
        xt_ref[...],
        nf[...].astype(BF16),
        (((1,), (1,)), ((), ())),
        preferred_element_type=F32,
    ).astype(BF16)
    for i in range(steps):
        part = pl.ds(i * block, block)
        left = l_refs[i][...].reshape(block, z2.shape[0])
        direction = jnp.dot(left, z2, preferred_element_type=F32)
        nw[part, :] = (w_ref[part, :].astype(F32) - scaled * direction).astype(BF16)
        copies.append(pltpu.make_async_copy(nw.at[part], nw_hbm.at[part], sems.at[2 * i + 1]))
        copies[-1].start()
    for c in copies:
        c.wait()


def local(nx, ny, nz, cols_total, scaled, gradient, momentum, right_factor, weight):
    n_rows, n_cols = gradient.shape
    rank = right_factor.shape[1]
    half = n_rows // CORES
    chips = nx * ny
    piece = chips * piece_rows
    n_pieces = half // piece
    plane = chips * CORES
    share = rank // plane
    part = rank // nz // sum_pieces
    block = n_rows // steps
    any_spec = pl.BlockSpec(memory_space=pl.ANY)
    vm_spec = pl.BlockSpec(memory_space=pltpu.VMEM)
    dma = pltpu.SemaphoreType.DMA
    vm = pltpu.VMEM
    shape = jax.ShapeDtypeStruct
    rows = (n_pieces, chips, piece_rows, rank)
    scratch = [
        vm((n_rows, n_cols), BF16),
        vm((n_rows, n_cols), BF16),
        vm((n_cols, rank), F32),
        vm((n_rows, n_cols), BF16),
        vm((n_pieces, piece, rank), BF16),
        vm((n_pieces, piece, rank), BF16),
        vm(rows, F32),
        vm(rows, BF16),
        vm(rows, BF16),
        vm((CORES,) + rows, BF16),
        vm((rank, n_rows), BF16),
        vm((rank, rank), F32),
        vm((nz, share, rank), F32),
        vm((rank, rank), F32),
        vm((rank, n_cols), F32),
        vm((nz, sum_pieces, part, n_cols), BF16),
        vm((sum_pieces, nz, part, n_cols), BF16),
        vm((nz, sum_pieces, part, n_cols), BF16),
        vm((rank, 2 * rank), F32),
        vm((rank, rank), F32),
        vm((plane, 2, rank // 2), F32),
        vm((rank, n_cols), BF16),
        vm((rank, rank), BF16),
        vm((n_cols, rank), F32),
        vm((8, rank), F32),
        dma((4 * n_pieces + 1,)),
        dma((2 * steps + 5,)),
    ]
    scratch += [dma((n_pieces,))] * 8
    scratch += [dma((nz - 1,)), dma((nz - 1,)), dma, dma]
    scratch += [dma((sum_pieces, nz - 1))] * 4 + [dma, dma]
    outs = [shape((block, n_cols), BF16)] * steps
    outs += [shape((block // piece_rows, piece_rows, rank), BF16)] * steps
    outs += [shape((rank, rank), BF16)]
    outs += [shape((n_cols // 2, rank), F32)] * 2 + [shape((8, rank), F32)]
    out = pl.pallas_call(
        functools.partial(factor_kernel, nx, ny, nz, cols_total),
        out_shape=outs,
        in_specs=[any_spec] * 3,
        out_specs=[any_spec] * len(outs),
        scratch_shapes=scratch,
        compiler_params=pltpu.CompilerParams(
            collective_id=0, has_side_effects=True, vmem_limit_bytes=51328 * 1024
        ),
        name="factors",
    )(gradient, momentum, right_factor)
    return pl.pallas_call(
        functools.partial(update_kernel, scaled),
        out_shape=[
            shape((n_rows, n_cols), BF16),
            shape((n_rows, n_cols), BF16),
            shape((n_cols, rank), F32),
        ],
        in_specs=[vm_spec] * (len(outs) + 1),
        out_specs=[any_spec] * 3,
        scratch_shapes=[
            vm((n_rows, n_cols), BF16),
            vm((n_cols, rank), F32),
            dma((2 * steps + 1,)),
        ],
        compiler_params=pltpu.CompilerParams(vmem_limit_bytes=16 * 1024 * 1024),
        name="update",
    )(*out[: 2 * steps], weight, *out[2 * steps :])


def build(mesh, nx, ny, nz, cols_total, rows_total, rank):
    scaled = step_size * (rows_total / rank) ** 0.5
    return jax.shard_map(
        functools.partial(local, nx, ny, nz, cols_total, scaled),
        mesh=mesh,
        in_specs=(P("row", "col"), P("row", "col"), P("col", None), P("row", "col")),
        out_specs=(P("row", "col"), P("row", "col"), P("col", None)),
        check_vma=False,
    )


def solution(mesh):
    return build(mesh, NX, NY, mesh.shape["row"], COLS, ROWS, RANK)
```

```python
import functools

import jax
import jax.numpy as jnp
from jax import lax
from jax.experimental import pallas as pl
from jax.experimental.pallas import tpu as pltpu
from jax.sharding import PartitionSpec as P

ROWS = 16384
COLS = 16384
RANK = 256
CORES = 2
sum_pieces = 2
piece_rows = 16
steps = 8
NX = 4
NY = 4

momentum_keep = 0.6
step_size = 0.1

F32 = jnp.float32
BF16 = jnp.bfloat16
MESH = pl.DeviceIdType.MESH


def split3(value):
    high = value.astype(BF16)
    rest = value - high.astype(F32)
    middle = rest.astype(BF16)
    return high, middle, (rest - middle.astype(F32)).astype(BF16)


def inverse_factor(gram_ref, work_ref, out_ref, size=32, group=16):
    n = gram_ref.shape[0]
    tiles_across = n // 128
    gram = gram_ref[...]
    rows = lax.broadcasted_iota(jnp.int32, (n, n), 0)
    cols = lax.broadcasted_iota(jnp.int32, (n, n), 1)
    diagonal = jnp.where(rows == cols, gram, 0.0)
    scale_row = lax.rsqrt(jnp.sum(diagonal, axis=0, keepdims=True))
    scale_col = lax.rsqrt(jnp.sum(diagonal, axis=1, keepdims=True))
    work_ref[:, :n] = gram * scale_row * scale_col

    def block(start):
        outer = start // 128 * 128
        lead = work_ref[start : start + size, outer : outer + 128]
        if start != outer:
            lead = pltpu.roll(lead, 128 - (start - outer), 1)
        panel = work_ref[start : start + size, :]
        used = [t for t in range(tiles_across) if (t + 1) * 128 > start]
        used += [tiles_across + t for t in range(tiles_across) if t * 128 < start + size]
        tiles = [lead] + [panel[:, t * 128 : (t + 1) * 128] for t in used]
        done = []
        for first in range(0, size, group):
            lead = tiles[0]
            columns = [
                jnp.broadcast_to(lead[:, first + i : first + i + 1], (size - first, 128))
                for i in range(group)
            ]
            for base in range(0, group, 8):
                sub = lax.broadcasted_iota(jnp.int32, (size - first - base, 128), 0)
                top = sub[:8]
                scale = jnp.ones((8, 128), F32)
                for k in range(0, 8, 2):
                    one, two = columns[base + k], columns[base + k + 1]
                    a = one[k : k + 1, :]
                    b = one[k + 1 : k + 2, :]
                    c = two[k + 1 : k + 2, :]
                    det = a * c - b * b
                    inv_a = 1.0 / a
                    inv_det = 1.0 / det
                    m1 = (one * c - two * b) * inv_det
                    m2 = (two * a - one * b) * inv_det
                    m1 = jnp.where(sub > k + 1, m1, jnp.where(sub == k + 1, b * inv_a, 0.0))
                    m2 = jnp.where(sub > k + 1, m2, 0.0)
                    scale = jnp.where(
                        top == k,
                        lax.rsqrt(a),
                        jnp.where(top == k + 1, lax.rsqrt(det * inv_a), scale),
                    )
                    for i in range(base + k + 2, group):
                        old = columns[i]
                        columns[i] = old - m1 * old[k : k + 1, :] - m2 * old[k + 1 : k + 2, :]
                    tiles = [t - m1 * t[k : k + 1, :] - m2 * t[k + 1 : k + 2, :] for t in tiles]
                done.append([t[:8] * scale for t in tiles[1:]])
                tiles = [t[8:] for t in tiles]
                columns = [c[8:] if i >= base + 8 else c for i, c in enumerate(columns)]
        found = {t: jnp.concatenate([d[i] for d in done], axis=0) for i, t in enumerate(used)}
        empty = jnp.zeros((size, 128), F32)
        tiles = [found.get(t, empty) for t in range(2 * tiles_across)]
        left = jnp.concatenate(tiles[:tiles_across], axis=1)
        right = jnp.concatenate(tiles[tiles_across:], axis=1)
        out_ref[start : start + size, :] = right * scale_row

        if start + size < n:
            lane = lax.broadcasted_iota(jnp.int32, (size, n), 1)
            rest = jnp.where(lane >= start + size, left, 0.0)
            ph, pm, pq = split3(rest)
            xh, xm, xq = split3(right)
            lhs = jnp.concatenate([ph, ph, pm, pm, ph, pq], axis=0)
            rhs_g = jnp.concatenate([ph, pm, ph, pm, pq, ph], axis=0)
            rhs_x = jnp.concatenate([xh, xm, xh, xm, xq, xh], axis=0)
            rhs = jnp.concatenate([rhs_g, rhs_x], axis=1)
            under = (start + size) // 128 * 128
            work_ref[under:, :] -= lax.dot_general(
                lhs[:, under:], rhs, (((0,), (0,)), ((), ())), preferred_element_type=F32
            )

    for start in range(0, n, size):
        block(start)


def factor_kernel(nx, ny, nz, cols_total, g_hbm, m_hbm, v_hbm, *refs):
    nm_outs, l_outs, refs = refs[:steps], refs[steps : 2 * steps], refs[2 * steps :]
    xt_out, r_out, r2_out, scale_out, g_v, m_v, v_v, b_v, xs, xr, s_v, sa, ra, la, *refs = refs
    lt, gfull, gz, gall, wacc, wh, wr, wg, work, inv, cs, z1, xt, right, scale_v, *refs = refs
    load_sem, out_sem, pair_s, pair_r, rs_s, rs_r, ag_s, ag_r, fw_s, fw_r, *refs = refs
    gz_s, gz_r, gp_s, gp_r, wr_s, wr_r, wg_s, wg_r, cs_s, cs_r = refs
    z = lax.axis_index("row")
    p = lax.axis_index("col")
    core = lax.rem(p, CORES)
    q = p // CORES
    chips = nx * ny
    plane = chips * CORES
    rank = v_v.shape[1]
    half_rank = rank // 2
    n_cols = b_v.shape[1]
    half = b_v.shape[0] // CORES
    n_pieces, piece = xs.shape[0], xs.shape[1]

    def at(chip_to, core_to):
        return {"row": z, "col": chip_to * CORES + core_to}

    sent = []

    def copy_to(src, dst, s_sem, r_sem, to):
        return pltpu.make_async_remote_copy(
            src_ref=src,
            dst_ref=dst,
            send_sem=s_sem,
            recv_sem=r_sem,
            device_id=to,
            device_id_type=MESH,
        )

    def send(src, dst, s_sem, r_sem, to):
        copy = copy_to(src, dst, s_sem, r_sem, to)
        copy.start()
        sent.append(copy)
        return copy

    v_load = pltpu.make_async_copy(v_hbm, v_v, load_sem.at[0])
    v_load.start()
    offsets = [(1 - core) * half + h * piece for h in range(n_pieces)]
    offsets += [core * half + h * piece for h in range(n_pieces)]
    offsets = [pl.multiple_of(o, piece) for o in offsets]
    loads = []
    for i, offset in enumerate(offsets):
        part = pl.ds(offset, piece)
        pair = [
            pltpu.make_async_copy(g_hbm.at[part], g_v.at[part], load_sem.at[2 * i + 1]),
            pltpu.make_async_copy(m_hbm.at[part], m_v.at[part], load_sem.at[2 * i + 2]),
        ]
        for c in pair:
            c.start()
        loads.append(pair)
    barrier = pltpu.get_barrier_semaphore()

    line_order = sorted(range(1, nz), key=lambda d: -min(d, nz - d))
    plane_far = (nx // 2 * ny + ny // 2) * CORES - 1
    chip_far = nx // 2 * ny + ny // 2 - 1

    def from_far(i, far, size):
        d = i + far
        return jnp.where(d >= size, d - (size - 1), d)

    def ring(here, d, size):
        to = here + d
        return jnp.where(to >= size, to - size, to)

    def greet_plane(d, carry):
        to = {"row": z, "col": ring(p, from_far(d, plane_far, plane), plane)}
        pl.semaphore_signal(barrier, inc=1, device_id=to, device_id_type=MESH)
        return carry

    def greet_line(d, carry):
        to = {"row": ring(z, d, nz), "col": p}
        pl.semaphore_signal(barrier, inc=1, device_id=to, device_id_type=MESH)
        return carry

    for d in line_order:
        greet_line(d, 0)
    for d in range(1, plane):
        greet_plane(d, 0)
    v_load.wait()
    factor_half = v_v[...].astype(BF16)

    def product(i):
        for c in loads[i]:
            c.wait()
        part = pl.ds(offsets[i], piece)
        blended = (m_v[part, :].astype(F32) + g_v[part, :].astype(F32)).astype(BF16)
        b_v[part, :] = blended
        return jnp.dot(blended, factor_half, preferred_element_type=F32)

    for h in range(n_pieces):
        xs[h] = product(h).astype(BF16)
    for h in range(n_pieces):
        s_v[h] = product(n_pieces + h).reshape(chips, piece_rows, rank)
        ra[h, q] = jnp.zeros((piece_rows, rank), BF16)
    pl.semaphore_wait(barrier, plane - 1 + nz - 1)
    pairs = []
    for h in range(n_pieces):
        pairs.append(send(xs.at[h], xr.at[h], pair_s.at[h], pair_r.at[h], at(q, 1 - core)))

    def spread_piece(h):
        def to_chip(d, carry):
            to = ring(q, from_far(d, chip_far, chips), chips)
            copy_to(sa.at[h, to], ra.at[h, q], rs_s.at[h], rs_r.at[h], at(to, core)).start()
            return carry

        lax.fori_loop(1, chips, to_chip, 0)

    for h in range(n_pieces):
        pairs[h].wait_recv()
        total = s_v[h] + xr[h].astype(F32).reshape(chips, piece_rows, rank)
        s_v[h] = total
        sa[h] = total.astype(BF16)
        spread_piece(h)

    def gather_piece(h):
        def to_chip(d, carry):
            to = ring(q, from_far(d, chip_far, chips), chips)
            here = la.at[core, h, q]
            copy_to(here, here, ag_s.at[h], ag_r.at[h], at(to, core)).start()
            return carry

        lax.fori_loop(1, chips, to_chip, 0)

    waits = []
    for h in range(n_pieces):
        slots = ra.at[h, pl.ds(0, chips - 1)]
        arrived = copy_to(slots, slots, rs_s.at[h], rs_r.at[h], at(q, 1 - core))
        arrived.wait_recv()
        waits.append(arrived)
        la[core, h, q] = (s_v[h, q] + jnp.sum(ra[h].astype(F32), axis=0)).astype(BF16)
        gather_piece(h)

    def accumulate(h):
        forwards[h].wait_recv()
        for c in range(CORES):
            rows = la[c, h].reshape(piece, rank)
            rows_t = rows.T
            first = (c * n_pieces + h) * piece
            lt[:, first : first + piece] = rows_t
            update = jnp.dot(rows_t, rows, preferred_element_type=F32)
            gfull[...] = update if h == 0 and c == 0 else gfull[...] + update

    def accumulate_right(h):
        for c in range(CORES):
            first = (c * n_pieces + h) * piece
            update = jnp.dot(
                lt[:, first : first + piece],
                b_v[first : first + piece, :],
                preferred_element_type=F32,
            )
            wacc[...] = update if h == 0 and c == 0 else wacc[...] + update

    forwards = []
    for h in range(n_pieces):
        slots = la.at[core, h, pl.ds(0, chips - 1)]
        arrived = copy_to(slots, slots, ag_s.at[h], ag_r.at[h], at(q, 1 - core))
        arrived.wait_recv()
        waits.append(arrived)
        here = la.at[core, h]
        forwards.append(send(here, here, fw_s.at[h], fw_r.at[h], at(q, 1 - core)))
        if h > 0:
            accumulate(h - 1)
            accumulate_right(h - 1)
    accumulate(n_pieces - 1)

    share = rank // plane
    mine = pl.ds(pl.multiple_of(p * share, share), share)
    gz[z] = gfull[mine, :]
    gz_c = []
    for d in line_order:
        to = {"row": ring(z, d, nz), "col": p}
        gz_c.append(send(gz.at[z], gz.at[z], gz_s.at[d - 1], gz_r.at[d - 1], to))

    accumulate_right(n_pieces - 1)
    w = wacc[...].astype(BF16)
    line = rank // nz
    part = line // sum_pieces
    wh[...] = w.reshape(nz, sum_pieces, part, n_cols)
    wr_c = []
    for h in range(sum_pieces):
        wr[h, z] = wh[z, h]
        for d in line_order:
            to = ring(z, d, nz)
            sems = wr_s.at[h, d - 1], wr_r.at[h, d - 1]
            wr_c.append(send(wh.at[to, h], wr.at[h, z], *sems, {"row": to, "col": p}))
    outs = []
    for i in range(steps):
        rows = b_v.shape[0] // steps
        c, h = i * rows // half, (i * rows % half) // piece
        chip = (i * rows % piece) // piece_rows
        source = la.at[c, h, pl.ds(chip, rows // piece_rows)]
        outs.append(pltpu.make_async_copy(source, l_outs[i], out_sem.at[2 * i]))
    for c in outs:
        c.start()

    for c in gz_c:
        c.wait_recv()
    acc = gz[0]
    for i in range(1, nz):
        acc = acc + gz[i]
    gall[mine, :] = acc

    def spread(d, carry):
        to = {"row": z, "col": ring(p, from_far(d, plane_far, plane), plane)}
        copy_to(gall.at[mine], gall.at[mine], gp_s, gp_r, to).start()
        return carry

    lax.fori_loop(1, plane, spread, 0)

    wg_c = []
    for h in range(sum_pieces):
        for c in wr_c[h * (nz - 1) : (h + 1) * (nz - 1)]:
            c.wait_recv()
        acc = wr[h, 0].astype(F32)
        for i in range(1, nz):
            acc = acc + wr[h, i].astype(F32)
        wg[z, h] = acc.astype(BF16)
        for d in line_order:
            to = {"row": ring(z, d, nz), "col": p}
            sems = wg_s.at[h, d - 1], wg_r.at[h, d - 1]
            wg_c.append(send(wg.at[z, h], wg.at[z, h], *sems, to))

    others = gall.at[pl.ds(0, (plane - 1) * share)]
    at_row = lax.broadcasted_iota(jnp.int32, (rank, rank), 0)
    at_col = lax.broadcasted_iota(jnp.int32, (rank, rank), 1)
    work[:, rank:] = jnp.where(at_row == at_col, 1.0, 0.0)
    all_gram = copy_to(others, others, gp_s, gp_r, at(q, 1 - core))
    all_gram.wait_recv()
    inverse_factor(gall, work, inv)

    for c in wg_c:
        c.wait_recv()
    w = wg[...].reshape(rank, n_cols)
    high, middle, _ = split3(inv[...])
    right_t = jnp.dot(high, w, preferred_element_type=F32) + jnp.dot(
        middle, w, preferred_element_type=F32
    )
    squares = right_t * right_t
    sq_h, sq_m, _ = split3(squares)
    ones = jnp.ones((8, n_cols), BF16)
    dims = (((1,), (1,)), ((), ()))
    sums = lax.dot_general(ones, sq_h, dims, preferred_element_type=F32) + lax.dot_general(
        ones, sq_m, dims, preferred_element_type=F32
    )
    cs[p] = jnp.concatenate([sums[0:1, :half_rank], sums[0:1, half_rank:]], axis=0)

    def spread_sums(d, carry):
        to = {"row": z, "col": ring(p, from_far(d, plane_far, plane), plane)}
        copy_to(cs.at[p], cs.at[p], cs_s, cs_r, to).start()
        return carry

    lax.fori_loop(1, plane, spread_sums, 0)
    inv_t = inv[...].T.astype(BF16)
    xt[...] = inv_t
    z1[...] = jnp.dot(inv_t, right_t.astype(BF16), preferred_element_type=F32).astype(BF16)
    right[...] = right_t.T
    mid = n_cols // 2
    outs += [
        pltpu.make_async_copy(xt, xt_out, out_sem.at[2 * steps + 1]),
        pltpu.make_async_copy(right.at[pl.ds(0, mid)], r_out, out_sem.at[2 * steps + 2]),
        pltpu.make_async_copy(right.at[pl.ds(mid, mid)], r2_out, out_sem.at[2 * steps + 3]),
    ]
    for c in outs[-3:]:
        c.start()
    rows = b_v.shape[0] // steps
    for i in range(steps):
        c, h = i * rows // half, (i * rows % half) // piece
        chip = (i * rows % piece) // piece_rows
        part = pl.ds(i * rows, rows)
        left = la[c, h, chip : chip + rows // piece_rows].reshape(rows, rank)
        projection = jnp.dot(left, z1[...], preferred_element_type=F32)
        b_v[part, :] = (b_v[part, :].astype(F32) - (1.0 - momentum_keep) * projection).astype(BF16)
        outs.append(pltpu.make_async_copy(b_v.at[part], nm_outs[i], out_sem.at[2 * i + 1]))
        outs[-1].start()
    for c in sent + waits + [all_gram]:
        c.wait_send()
    other_sums = cs.at[pl.ds(0, plane - 1)]
    all_sums = copy_to(other_sums, other_sums, cs_s, cs_r, at(q, 1 - core))
    all_sums.wait_recv()
    acc = cs[0]
    for i in range(1, plane):
        acc = acc + cs[i]
    acc = lax.rsqrt(acc / cols_total + 1e-06)
    scale = jnp.concatenate([acc[0:1, :], acc[1:2, :]], axis=1)
    scale_v[...] = jnp.broadcast_to(scale, scale_v.shape)
    outs.append(pltpu.make_async_copy(scale_v, scale_out, out_sem.at[2 * steps + 4]))
    outs[-1].start()
    for c in outs:
        c.wait()
    all_sums.wait_send()


def update_kernel(scaled, *refs):
    nm_refs, l_refs, refs = refs[:steps], refs[steps : 2 * steps], refs[2 * steps :]
    w_ref, xt_ref, r_ref, r2_ref, scale_ref, nw_hbm, nm_hbm, nf_hbm, nw, nf, sems = refs
    block = nw.shape[0] // steps
    mid = r_ref.shape[0]
    copies = []
    for i in range(steps):
        part = pl.ds(i * block, block)
        copies.append(pltpu.make_async_copy(nm_refs[i], nm_hbm.at[part], sems.at[2 * i]))
        copies[-1].start()
    scale = scale_ref[0:1, :]
    nf[:mid, :] = r_ref[...] * scale
    nf[mid:, :] = r2_ref[...] * scale
    copies.append(pltpu.make_async_copy(nf, nf_hbm, sems.at[2 * steps]))
    copies[-1].start()
    z2 = lax.dot_general(
        xt_ref[...],
        nf[...].astype(BF16),
        (((1,), (1,)), ((), ())),
        preferred_element_type=F32,
    ).astype(BF16)
    for i in range(steps):
        part = pl.ds(i * block, block)
        left = l_refs[i][...].reshape(block, z2.shape[0])
        direction = jnp.dot(left, z2, preferred_element_type=F32)
        nw[part, :] = (w_ref[part, :].astype(F32) - scaled * direction).astype(BF16)
        copies.append(pltpu.make_async_copy(nw.at[part], nw_hbm.at[part], sems.at[2 * i + 1]))
        copies[-1].start()
    for c in copies:
        c.wait()


def local(nx, ny, nz, cols_total, scaled, gradient, momentum, right_factor, weight):
    n_rows, n_cols = gradient.shape
    rank = right_factor.shape[1]
    half = n_rows // CORES
    chips = nx * ny
    piece = chips * piece_rows
    n_pieces = half // piece
    plane = chips * CORES
    share = rank // plane
    part = rank // nz // sum_pieces
    block = n_rows // steps
    any_spec = pl.BlockSpec(memory_space=pl.ANY)
    vm_spec = pl.BlockSpec(memory_space=pltpu.VMEM)
    dma = pltpu.SemaphoreType.DMA
    vm = pltpu.VMEM
    shape = jax.ShapeDtypeStruct
    rows = (n_pieces, chips, piece_rows, rank)
    scratch = [
        vm((n_rows, n_cols), BF16),
        vm((n_rows, n_cols), BF16),
        vm((n_cols, rank), F32),
        vm((n_rows, n_cols), BF16),
        vm((n_pieces, piece, rank), BF16),
        vm((n_pieces, piece, rank), BF16),
        vm(rows, F32),
        vm(rows, BF16),
        vm(rows, BF16),
        vm((CORES,) + rows, BF16),
        vm((rank, n_rows), BF16),
        vm((rank, rank), F32),
        vm((nz, share, rank), F32),
        vm((rank, rank), F32),
        vm((rank, n_cols), F32),
        vm((nz, sum_pieces, part, n_cols), BF16),
        vm((sum_pieces, nz, part, n_cols), BF16),
        vm((nz, sum_pieces, part, n_cols), BF16),
        vm((rank, 2 * rank), F32),
        vm((rank, rank), F32),
        vm((plane, 2, rank // 2), F32),
        vm((rank, n_cols), BF16),
        vm((rank, rank), BF16),
        vm((n_cols, rank), F32),
        vm((8, rank), F32),
        dma((4 * n_pieces + 1,)),
        dma((2 * steps + 5,)),
    ]
    scratch += [dma((n_pieces,))] * 8
    scratch += [dma((nz - 1,)), dma((nz - 1,)), dma, dma]
    scratch += [dma((sum_pieces, nz - 1))] * 4 + [dma, dma]
    outs = [shape((block, n_cols), BF16)] * steps
    outs += [shape((block // piece_rows, piece_rows, rank), BF16)] * steps
    outs += [shape((rank, rank), BF16)]
    outs += [shape((n_cols // 2, rank), F32)] * 2 + [shape((8, rank), F32)]
    out = pl.pallas_call(
        functools.partial(factor_kernel, nx, ny, nz, cols_total),
        out_shape=outs,
        in_specs=[any_spec] * 3,
        out_specs=[any_spec] * len(outs),
        scratch_shapes=scratch,
        compiler_params=pltpu.CompilerParams(
            collective_id=0, has_side_effects=True, vmem_limit_bytes=51328 * 1024
        ),
        name="factors",
    )(gradient, momentum, right_factor)
    return pl.pallas_call(
        functools.partial(update_kernel, scaled),
        out_shape=[
            shape((n_rows, n_cols), BF16),
            shape((n_rows, n_cols), BF16),
            shape((n_cols, rank), F32),
        ],
        in_specs=[vm_spec] * (len(outs) + 1),
        out_specs=[any_spec] * 3,
        scratch_shapes=[
            vm((n_rows, n_cols), BF16),
            vm((n_cols, rank), F32),
            dma((2 * steps + 1,)),
        ],
        compiler_params=pltpu.CompilerParams(vmem_limit_bytes=16 * 1024 * 1024),
        name="update",
    )(*out[: 2 * steps], weight, *out[2 * steps :])


def build(mesh, nx, ny, nz, cols_total, rows_total, rank):
    scaled = step_size * (rows_total / rank) ** 0.5
    return jax.shard_map(
        functools.partial(local, nx, ny, nz, cols_total, scaled),
        mesh=mesh,
        in_specs=(P("row", "col"), P("row", "col"), P("col", None), P("row", "col")),
        out_specs=(P("row", "col"), P("row", "col"), P("col", None)),
        check_vma=False,
    )


def solution(mesh):
    return build(mesh, NX, NY, mesh.shape["row"], COLS, ROWS, RANK)
```
